256 devices in a mesh: prefix: 8 (over z_hi, core), replica: 8 (over z_lo, x), tensor: 4 (over y).
Axes of the slice: x: 4, y: 4, z: 8 (z_hi: 4, z_lo: 2; z = z_hi * 2 + z_lo), core: 2. Of those that a mesh axis runs over, the one named last changes fastest.
Arguments:
- queries: bfloat16 [4, 64, 8192], P(None, ('prefix', 'replica'), 'tensor'), may hold values from -8 to 8
- common_prefix_keys: bfloat16 [196608, 1024], P(('prefix', 'replica'), 'tensor'), may hold values from -12 to 12
- common_prefix_values: bfloat16 [196608, 1024], P(('prefix', 'replica'), 'tensor'), may hold values from -6 to 6
- branch_suffix_keys: bfloat16 [64, 1024, 1024], P(('prefix', 'replica'), None, 'tensor'), may hold values from -12 to 12
- branch_suffix_values: bfloat16 [64, 1024, 1024], P(('prefix', 'replica'), None, 'tensor'), may hold values from -6 to 6
- position_keys: bfloat16 [4, 64, 1024], P(None, ('prefix', 'replica'), 'tensor'), may hold values from -12 to 12
- position_values: bfloat16 [4, 64, 1024], P(None, ('prefix', 'replica'), 'tensor'), may hold values from -6 to 6
- lengths: int32 [64], P(('prefix', 'replica')), may hold values from 1 to 1024, 32768 in all
- out_weight: bfloat16 [8192, 5120], P('tensor', ('prefix', 'replica')), may hold values from -0.0625 to 0.0625
Outputs:
- projected: bfloat16 [4, 64, 5120], P(None, 'tensor', ('prefix', 'replica'))
The draws below stay inside these ranges and needn't reach their ends.
Inputs may be any that keep to these rules, and one draw needn't show every extreme that they name: The lengths sum to 32768 and the largest is exactly 1024.
All inputs are finite; a program needn't handle non-finite values. No bound on the sum of `lengths` on one device may be relied on, other than what follows from the above.
Results may differ from the reference program's by a relative error of at most 0.015.
Values may be sent and summed in bfloat16 or wider, within the bound.
No kernel may reach another device: no remote copies, remote signals or barrier semaphores. Data moves between devices by JAX's collectives and lax.ppermute only.
A program may use at most 64 MiB of HBM per device.

```python
import math
import jax
import jax.numpy as jnp
import numpy as np
from jax import lax

D = 5120
QUERY_HEADS = 64
KEY_VALUE_HEADS = 8
HEAD_SIZE = 128
NEW_POSITIONS = 4
PREFIX_PER_SHARD = 3072
SUFFIX_SLOTS = 1024
BRANCH_TOTAL = 64
PREFIX_LENGTH = 196608
N_PREFIX = 8
N_REPLICA = 8


def shared_direction(key):
    return jnp.clip(jax.random.normal(jax.random.fold_in(key, 101), (BRANCH_TOTAL, KEY_VALUE_HEADS, HEAD_SIZE), jnp.float32), -4.0, 4.0)


def per_row_scale(key, shape_rows):
    return jnp.exp(jax.random.uniform(key, shape_rows, jnp.float32, math.log(0.2), math.log(2.0)))


def random_noise(key, shape_all):
    return jnp.clip(jax.random.normal(key, shape_all, jnp.float32), -4.0, 4.0)


def draw_queries(key, part):
    direction_vectors = shared_direction(key)
    key = jax.random.fold_in(key, 1)
    leading_key = jax.random.fold_in(key, 0)
    query_group_width = QUERY_HEADS // KEY_VALUE_HEADS
    noise_matrix_rows = jnp.clip(jax.random.normal(leading_key, (NEW_POSITIONS, BRANCH_TOTAL, KEY_VALUE_HEADS, query_group_width, HEAD_SIZE), jnp.float32), -4.0, 4.0)
    final_output = noise_matrix_rows + 0.7 * direction_vectors[None, :, :, None, :]
    return final_output.reshape(NEW_POSITIONS, BRANCH_TOTAL, QUERY_HEADS * HEAD_SIZE).astype(jnp.bfloat16)


def draw_common_prefix_keys(key, part):
    key = jax.random.fold_in(key, 2)
    leading_key, following_key = jax.random.split(key, 2)
    final_output = per_row_scale(leading_key, (PREFIX_LENGTH, 1)) * random_noise(following_key, (PREFIX_LENGTH, KEY_VALUE_HEADS * HEAD_SIZE))
    return final_output.astype(jnp.bfloat16)


def draw_branch_suffix_keys(key, part):
    direction_vectors = shared_direction(key)
    key = jax.random.fold_in(key, 3)
    leading_key, following_key = jax.random.split(key, 2)
    final_output = per_row_scale(leading_key, (BRANCH_TOTAL, SUFFIX_SLOTS, 1, 1)) * random_noise(following_key, (BRANCH_TOTAL, SUFFIX_SLOTS, KEY_VALUE_HEADS, HEAD_SIZE))
    final_output = final_output + 0.7 * direction_vectors[:, None, :, :]
    return final_output.reshape(BRANCH_TOTAL, SUFFIX_SLOTS, KEY_VALUE_HEADS * HEAD_SIZE).astype(jnp.bfloat16)


def draw_position_keys(key, part):
    direction_vectors = shared_direction(key)
    key = jax.random.fold_in(key, 4)
    final_output = random_noise(key, (NEW_POSITIONS, BRANCH_TOTAL, KEY_VALUE_HEADS, HEAD_SIZE)) + 1.5 * direction_vectors[None, :, :, :]
    return final_output.reshape(NEW_POSITIONS, BRANCH_TOTAL, KEY_VALUE_HEADS * HEAD_SIZE).astype(jnp.bfloat16)


def levels(own_key, dims, shards, low, largest):
    factor_of, own = 1.0, jax.random.fold_in(own_key, 6)
    for dim, shards_of in shards:
        heights = jnp.exp(jax.random.uniform(jax.random.fold_in(own, dim), (shards_of,), jnp.float32, low / len(shards), largest / len(shards)))
        factor_of = factor_of * jnp.repeat(heights, dims[dim] // shards_of).reshape([-1 if axis == dim else 1 for axis in range(len(dims))])
    return factor_of


def length_profile(number_of, total, limit, skew):
    loads = [(1 << 20) // math.isqrt(grade ** skew) + 1 for grade in range(2, number_of + 1)]
    spare, counts = total - limit - (number_of - 1), [1] * (number_of - 1)
    while spare > 0:
        candidates = [i for i in range(number_of - 1) if counts[i] < limit]
        mass, budget = sum([loads[i] for i in candidates]), spare
        for i in candidates:
            more = min(limit - counts[i], max(1, budget * loads[i] // mass), spare)
            counts[i] = counts[i] + more
            spare = spare - more
    return np.array([limit] + counts)


def ragged_sizes(key, count, total, bound, slope):
    if count == 2:
        one = jax.random.randint(key, (), max(1, total - bound), min(bound, total - 1) + 1)
        return jnp.stack([one, total - one])
    sizes = jnp.asarray(length_profile(count, total, bound, slope), jnp.int32)
    couples = (count - 1) // 2
    source_of, receiver = sizes[1:1 + 2 * couples:2], sizes[2:2 + 2 * couples:2]
    slack = jnp.minimum(source_of - 1, bound - receiver)
    passed = jax.random.randint(jax.random.fold_in(key, 1), (couples,), 0, 1 << 20) % (slack + 1)
    sizes = sizes.at[1:1 + 2 * couples:2].set(source_of - passed).at[2:2 + 2 * couples:2].set(receiver + passed)
    return sizes[jax.random.permutation(jax.random.fold_in(key, 2), count)]


def noise(rng, extent, deviation, limit, cuts=(), kind=jnp.bfloat16):
    level = levels(rng, extent, cuts, -0.22, 0.18) if cuts else 1.0
    drawn = jax.random.normal(rng, extent, jnp.float32) * deviation * level
    return jnp.minimum(jnp.maximum(drawn, -limit), limit).astype(kind)


def setup_inputs(seed: int = 0) -> dict:
    keys = jax.random.split(jax.random.key(seed), 10)
    return {
        "queries": draw_queries(jax.random.fold_in(keys[9], 71), 0),
        "common_prefix_keys": draw_common_prefix_keys(jax.random.fold_in(keys[9], 71), 0),
        "common_prefix_values": noise(keys[2], (PREFIX_LENGTH, KEY_VALUE_HEADS * HEAD_SIZE), 1.0, 6.0, ((0, 64), (1, 4))),
        "branch_suffix_keys": draw_branch_suffix_keys(jax.random.fold_in(keys[9], 71), 0),
        "branch_suffix_values": noise(keys[4], (BRANCH_TOTAL, SUFFIX_SLOTS, KEY_VALUE_HEADS * HEAD_SIZE), 1.0, 6.0, ((0, 64), (2, 4))),
        "position_keys": draw_position_keys(jax.random.fold_in(keys[9], 71), 0),
        "position_values": noise(keys[6], (NEW_POSITIONS, BRANCH_TOTAL, KEY_VALUE_HEADS * HEAD_SIZE), 1.0, 6.0, ((1, 64), (2, 4))),
        "lengths": ragged_sizes(keys[7], BRANCH_TOTAL, BRANCH_TOTAL * SUFFIX_SLOTS // 2, SUFFIX_SLOTS, 2).astype(jnp.int32),
        "out_weight": noise(keys[8], (QUERY_HEADS * HEAD_SIZE, D), (QUERY_HEADS * HEAD_SIZE) ** -0.5, 0.0625, ((0, 4), (1, 64))),
    }


def reference(queries, common_prefix_keys, common_prefix_values, branch_suffix_keys, branch_suffix_values, position_keys, position_values, lengths, out_weight):
    query_group_width = QUERY_HEADS // KEY_VALUE_HEADS
    score_scale = HEAD_SIZE ** -0.5
    number_of_blocks = N_PREFIX * N_REPLICA
    number_of_rows = NEW_POSITIONS * BRANCH_TOTAL
    query_matrix = queries.astype(jnp.float32).reshape(number_of_rows, KEY_VALUE_HEADS, query_group_width, HEAD_SIZE)
    blocked_keys = common_prefix_keys.reshape(number_of_blocks, PREFIX_PER_SHARD, KEY_VALUE_HEADS, HEAD_SIZE)
    blocked_values = common_prefix_values.reshape(number_of_blocks, PREFIX_PER_SHARD, KEY_VALUE_HEADS, HEAD_SIZE)

    def fold_block(state_carry, kv_block):
        run_max, run_total, run_sum = state_carry
        keys_blk, values_blk = kv_block
        scores = jnp.einsum('rgqd,kgd->rgqk', query_matrix, keys_blk.astype(jnp.float32)) * score_scale
        block_max = jnp.max(scores, axis=-1)
        weights = jnp.exp(scores - block_max[..., None])
        block_total = jnp.sum(weights, axis=-1)
        block_weights = lax.optimization_barrier(weights.astype(jnp.bfloat16))
        block_out = jnp.einsum('rgqk,kgd->rgqd', block_weights.astype(jnp.float32), values_blk.astype(jnp.float32)) / block_total[..., None]
        block_lse = block_max + jnp.log(block_total)
        new_max = jnp.maximum(run_max, block_lse)
        rescale = jnp.exp(run_max - new_max)
        take_part = jnp.exp(block_lse - new_max)
        return (new_max, run_total * rescale + take_part, run_sum * rescale[..., None] + take_part[..., None] * block_out), None

    initial_state = (jnp.full((number_of_rows, KEY_VALUE_HEADS, query_group_width), -jnp.inf, jnp.float32),
                   jnp.zeros((number_of_rows, KEY_VALUE_HEADS, query_group_width), jnp.float32),
                   jnp.zeros((number_of_rows, KEY_VALUE_HEADS, query_group_width, HEAD_SIZE), jnp.float32))
    (prefix_maximum, prefix_weighted_total, prefix_exp_sum), unused = lax.scan(fold_block, initial_state, (blocked_keys, blocked_values))
    prefix_maximum = prefix_maximum.reshape(NEW_POSITIONS, BRANCH_TOTAL, KEY_VALUE_HEADS, query_group_width)
    prefix_weighted_total = prefix_weighted_total.reshape(NEW_POSITIONS, BRANCH_TOTAL, KEY_VALUE_HEADS, query_group_width)
    prefix_exp_sum = prefix_exp_sum.reshape(NEW_POSITIONS, BRANCH_TOTAL, KEY_VALUE_HEADS, query_group_width, HEAD_SIZE)

    query_offsets = queries.astype(jnp.float32).reshape(NEW_POSITIONS, BRANCH_TOTAL, KEY_VALUE_HEADS, query_group_width, HEAD_SIZE)
    stored_keys = branch_suffix_keys.astype(jnp.float32).reshape(BRANCH_TOTAL, SUFFIX_SLOTS, KEY_VALUE_HEADS, HEAD_SIZE)
    stored_values = branch_suffix_values.astype(jnp.float32).reshape(BRANCH_TOTAL, SUFFIX_SLOTS, KEY_VALUE_HEADS, HEAD_SIZE)
    recent_keys = position_keys.astype(jnp.float32).reshape(NEW_POSITIONS, BRANCH_TOTAL, KEY_VALUE_HEADS, HEAD_SIZE)
    recent_values = position_values.astype(jnp.float32).reshape(NEW_POSITIONS, BRANCH_TOTAL, KEY_VALUE_HEADS, HEAD_SIZE)
    suffix_scores = jnp.einsum('pbgqd,btgd->pbgqt', query_offsets, stored_keys) * score_scale
    visible = jnp.arange(SUFFIX_SLOTS, dtype=jnp.int32)[None, :] < lengths[:, None]
    suffix_scores = jnp.where(visible[None, :, None, None, :], suffix_scores, -jnp.inf)
    fresh_scores = jnp.einsum('pbgqd,jbgd->pbgqj', query_offsets, recent_keys) * score_scale
    causal = jnp.arange(NEW_POSITIONS, dtype=jnp.int32)[None, :] <= jnp.arange(NEW_POSITIONS, dtype=jnp.int32)[:, None]
    fresh_scores = jnp.where(causal[:, None, None, None, :], fresh_scores, -jnp.inf)
    own_max = jnp.maximum(jnp.max(suffix_scores, axis=-1), jnp.max(fresh_scores, axis=-1))
    suffix_weights = jnp.exp(suffix_scores - own_max[..., None])
    fresh_weights = jnp.exp(fresh_scores - own_max[..., None])
    own_total = jnp.sum(suffix_weights, axis=-1) + jnp.sum(fresh_weights, axis=-1)
    suffix_low = lax.optimization_barrier(suffix_weights.astype(jnp.bfloat16))
    fresh_low = lax.optimization_barrier(fresh_weights.astype(jnp.bfloat16))
    own_sum = jnp.einsum('pbgqt,btgd->pbgqd', suffix_low.astype(jnp.float32), stored_values)
    own_sum = own_sum + jnp.einsum('pbgqj,jbgd->pbgqd', fresh_low.astype(jnp.float32), recent_values)

    combined_max = jnp.maximum(own_max, prefix_maximum)
    own_factor = jnp.exp(own_max - combined_max)
    far_factor = jnp.exp(prefix_maximum - combined_max)
    numer = own_sum * own_factor[..., None] + prefix_exp_sum * far_factor[..., None]
    denom = own_total * own_factor + prefix_weighted_total * far_factor
    attention = (numer / denom[..., None]).astype(jnp.bfloat16).reshape(number_of_rows, QUERY_HEADS * HEAD_SIZE)
    projected = jnp.dot(attention, out_weight, preferred_element_type=jnp.float32)
    return projected.astype(jnp.bfloat16).reshape(NEW_POSITIONS, BRANCH_TOTAL, D)
```

```python
import functools

import jax
import jax.numpy as jnp
from jax import lax
from jax.experimental import pallas as pl
from jax.experimental.pallas import tpu as pltpu
from jax.sharding import PartitionSpec as P

HEAD = 128
LOG2_SCALE = HEAD ** (-0.5) * 1.4426950408889634
NX, NZ = 4, 8
F32, BF16 = jnp.float32, jnp.bfloat16
PLANE = ("prefix", "replica")
VMEM = pl.BlockSpec(memory_space=pltpu.VMEM)
SMEM = pl.BlockSpec(memory_space=pltpu.SMEM)


def params(mib=8):
    return pltpu.CompilerParams(vmem_limit_bytes=mib << 20)


def plane_index(x, z, core):
    return ((z // 2) * 2 + core) * 8 + (z % 2) * 4 + x


ZC_GROUPS = [[plane_index(x, z, c) for z in range(NZ) for c in range(2)] for x in range(NX)]
CORE_SWAP = [(p, p ^ 1) for p in range(8)]


Z_PARTNERS = (
    [z ^ 1 for z in range(NZ)],
    [(z - 1) % NZ if z % 2 == 0 else (z + 1) % NZ for z in range(NZ)],
    [(z + 3) % NZ if z % 2 == 0 else (z - 3) % NZ for z in range(NZ)],
)


def z_exchange(step):
    return [
        (plane_index(x, z, c), plane_index(x, Z_PARTNERS[step][z], c))
        for x in range(NX)
        for z in range(NZ)
        for c in range(2)
    ]


def x_shift(k):
    return [(zl * 4 + x, zl * 4 + (x + k) % 4) for zl in range(2) for x in range(4)]


ROWS = NZ * 64
PACKED = (ROWS + 16, HEAD)


def eye():
    return lax.broadcasted_iota(jnp.int32, (HEAD, HEAD), 0) == lax.broadcasted_iota(
        jnp.int32, (HEAD, HEAD), 1
    )


def pack(o_ref, parts):
    rows = []
    for i, (out, lse) in enumerate(parts):
        o_ref[i * HEAD : (i + 1) * HEAD, :] = out.astype(BF16)
        rows.append(jnp.sum(jnp.where(eye(), lse, 0.0), axis=0, keepdims=True))
    rows = jnp.concatenate(rows, axis=0)
    high = rows.astype(BF16).astype(F32)
    middle = (rows - high).astype(BF16).astype(F32)
    low = rows - high - middle
    stats = jnp.concatenate([high, middle, low, jnp.zeros_like(low)], axis=0)
    o_ref[ROWS:, :] = stats.astype(BF16)


def unpack(ref):
    stats = ref[ROWS:, :].astype(F32)
    rows = stats[0:4] + stats[4:8] + stats[8:12]
    parts = []
    for i in range(4):
        lse = jnp.sum(jnp.where(eye(), rows[i : i + 1], 0.0), axis=1, keepdims=True)
        parts.append((ref[i * HEAD : (i + 1) * HEAD, :].astype(F32), lse))
    return parts


def merge(parts):
    top = functools.reduce(jnp.maximum, [lse for _, lse in parts])
    factors = [jnp.exp2(lse - top) for _, lse in parts]
    total = functools.reduce(jnp.add, factors)
    summed = functools.reduce(jnp.add, [f * out for f, (out, _) in zip(factors, parts)])
    return summed / total, top + jnp.log2(total)


def query_kernel(q_ref, o_ref, flat_ref):
    q = q_ref[...].astype(F32)
    rows = jnp.concatenate([q[:, i * HEAD : (i + 1) * HEAD] for i in range(16)], axis=0)
    rows = rows.astype(BF16)
    flat_ref[...] = rows
    for z in range(NZ):
        o_ref[z] = rows


def arrange_kernel(core_ref, k_ref, v_ref, send_ref, sems):
    columns = pl.ds(pl.multiple_of((1 - core_ref[0]) * HEAD, HEAD), HEAD)
    copies = [
        pltpu.make_async_copy(
            ref.at[:, columns], send_ref.at[:, pl.ds(i * HEAD, HEAD)], sems.at[i]
        )
        for i, ref in enumerate((k_ref, v_ref))
    ]
    for copy in copies:
        copy.start()
    for copy in copies:
        copy.wait()


def suffix_kernel(length_ref, core_ref, q_ref, k_ref, v_ref, nk_ref, nv_ref, own_ref, send_ref):
    length = length_ref[0]
    slots = k_ref.shape[0]
    visible = lax.broadcasted_iota(jnp.int32, (32, slots), 1) < length
    new_row = lax.broadcasted_iota(jnp.int32, (32, 16), 0) % 4
    new_col = lax.broadcasted_iota(jnp.int32, (32, 16), 1)
    causal = new_col <= new_row
    nt = (((1,), (1,)), ((), ()))
    empty = jnp.zeros((12, 2 * HEAD), F32)
    new_keys = jnp.concatenate([nk_ref[...].astype(F32), empty], axis=0).astype(BF16)
    new_values = jnp.concatenate([nv_ref[...].astype(F32), empty], axis=0).astype(BF16)
    results = []
    for g in range(2):
        columns = slice(g * HEAD, (g + 1) * HEAD)
        q = q_ref[g * 32 : (g + 1) * 32, :]
        s = lax.dot_general(q, k_ref[:, columns], nt, preferred_element_type=F32)
        t = lax.dot_general(q, new_keys[:, columns], nt, preferred_element_type=F32)
        s = jnp.where(visible, s * LOG2_SCALE, -jnp.inf)
        t = jnp.where(causal, t * LOG2_SCALE, -jnp.inf)
        top = jnp.maximum(
            jnp.max(s, axis=1, keepdims=True), jnp.max(t, axis=1, keepdims=True)
        )
        ws, wt = jnp.exp2(s - top), jnp.exp2(t - top)
        total = jnp.sum(ws, axis=1, keepdims=True) + jnp.sum(wt, axis=1, keepdims=True)
        summed = jnp.dot(ws.astype(BF16), v_ref[:, columns], preferred_element_type=F32)
        summed += jnp.dot(wt.astype(BF16), new_values[:, columns], preferred_element_type=F32)
        lse = jnp.broadcast_to(top + jnp.log2(total), (32, HEAD))
        results.append(jnp.concatenate([summed / total, lse], axis=0))
    first = core_ref[0] == 0
    own_ref[...] = jnp.where(first, results[0], results[1])
    send_ref[...] = jnp.where(first, results[1], results[0])


def fetch_kernel(away_ref, o_ref, sem):
    copy = pltpu.make_async_copy(away_ref, o_ref, sem)
    copy.start()
    copy.wait()


def attend_kernel(span, core_ref, q_ref, k_ref, v_ref, other_ref, o_ref):
    q = q_ref[...].reshape(NZ * 64, HEAD)
    top = summed = None
    mine = pl.ds(pl.multiple_of(core_ref[0] * HEAD, HEAD), HEAD)
    ones = jnp.ones((span, HEAD), BF16)
    sources = ((k_ref, mine, v_ref, mine), (other_ref, pl.ds(0, HEAD), other_ref, pl.ds(HEAD, HEAD)))
    for keys, key_columns, values, value_columns in sources:
        for start in range(0, keys.shape[0], span):
            rows = pl.ds(start, span)
            s = lax.dot_general(
                q,
                keys[rows, key_columns],
                (((1,), (1,)), ((), ())),
                preferred_element_type=F32,
            )
            here = jnp.max(s, axis=1, keepdims=True)
            new_top = here if top is None else jnp.maximum(top, here)
            w = jnp.exp2((s - new_top) * LOG2_SCALE).astype(BF16)
            widened = jnp.concatenate([values[rows, value_columns], ones], axis=1)
            part = jnp.dot(w, widened, preferred_element_type=F32)
            if top is None:
                summed = part
            else:
                summed = summed * jnp.exp2((top - new_top) * LOG2_SCALE) + part
            top = new_top
    total = summed[:, HEAD:]
    out = summed[:, :HEAD] / total
    lse = top * LOG2_SCALE + jnp.log2(total)
    blocks = [slice(i * HEAD, (i + 1) * HEAD) for i in range(4)]
    pack(o_ref, [(out[rows], lse[rows]) for rows in blocks])


def merge_kernel(z_ref, core_ref, a_ref, b_ref, c_ref, d_ref, own_ref, sibling_ref, o_ref):
    own, sibling = own_ref[...], sibling_ref[...]
    first = core_ref[0] == 0
    low, high = jnp.where(first, own, sibling), jnp.where(first, sibling, own)
    near_out = jnp.concatenate([low[0:32], high[0:32]] * 2, axis=0)
    near_lse = jnp.concatenate([low[32:], high[32:]] * 2, axis=0)
    half = lax.broadcasted_iota(jnp.int32, (HEAD, HEAD), 0) // 64
    far = [unpack(ref) for ref in (a_ref, b_ref, c_ref, d_ref)]
    merged = []
    for i in range(4):
        here = jnp.where(half + 2 * i == z_ref[0], near_lse, -jnp.inf)[:, 0:1]
        merged.append(merge([part[i] for part in far] + [(near_out, here)]))
    pack(o_ref, merged)


def pair_kernel(a_ref, b_ref, o_ref):
    pack(o_ref, [merge(list(parts)) for parts in zip(unpack(a_ref), unpack(b_ref))])


def finish_kernel(a_ref, b_ref, o_ref):
    rows = []
    for parts in zip(unpack(a_ref), unpack(b_ref)):
        out, _ = merge(list(parts))
        for start in (0, 64):
            heads = [
                jnp.concatenate(
                    [
                        out[start + h * 4 : start + h * 4 + 4],
                        out[start + 32 + h * 4 : start + 36 + h * 4],
                    ],
                    axis=0,
                )
                for h in range(8)
            ]
            rows.append(jnp.concatenate(heads, axis=1))
    o_ref[...] = jnp.concatenate(rows, axis=0).astype(BF16)


def project_kernel(x_ref, core_ref, a_ref, b_ref, c_ref, d_ref, w_ref, ws_ref, own_ref, send_ref):
    nt = (((1,), (1,)), ((), ()))
    width = ws_ref.shape[1]
    mine = w_ref[:, pl.ds(pl.multiple_of(core_ref[0] * width, width), width)]
    other = ws_ref[...]
    for k, ref in enumerate((a_ref, b_ref, c_ref, d_ref)):
        place = lax.rem(x_ref[0] + k, NX)
        rows = ref[...]
        for weight, o_ref in ((mine, own_ref), (other, send_ref)):
            product = lax.dot_general(rows, weight, nt, preferred_element_type=F32)
            product = product.astype(BF16)
            for t in range(4):
                o_ref[t, place] = product[t * 16 : (t + 1) * 16]


def halve_kernel(t_ref, a_ref, b_ref, keep_ref, send_ref):
    t = t_ref[0]
    partner = t + 1 - 2 * lax.rem(t, 2)
    for ref, owner in ((keep_ref, t), (send_ref, partner)):
        for i, block in enumerate((owner, 3 - owner)):
            ref[i] = (a_ref[block].astype(F32) + b_ref[block].astype(F32)).astype(BF16)


def quarter_kernel(a_ref, b_ref, keep_ref, send_ref):
    keep_ref[...] = a_ref[0].astype(F32) + b_ref[0].astype(F32)
    send_ref[...] = (a_ref[1].astype(F32) + b_ref[1].astype(F32)).astype(BF16)


def sum_kernel(a_ref, b_ref, o_ref):
    total = (a_ref[...] + b_ref[...].astype(F32)).reshape(64, a_ref.shape[2])
    row = lax.broadcasted_iota(jnp.int32, (64, 64), 0)
    column = lax.broadcasted_iota(jnp.int32, (64, 64), 1)
    source = (row % 4) * 16 + ((row // 4) % 2) * 8 + ((row // 8) % 2) * 4 + row // 16
    moved = jnp.dot(
        (column == source).astype(BF16), total.astype(BF16), preferred_element_type=F32
    ).astype(BF16)
    for p in range(4):
        o_ref[p] = moved[p * 16 : (p + 1) * 16]


def call(kernel, shapes, specs, name, flops=0, moved=0, exps=0, mib=8, scratch=()):
    return pl.pallas_call(
        kernel,
        out_shape=shapes,
        in_specs=specs,
        out_specs=jax.tree.map(lambda _: VMEM, shapes),
        scratch_shapes=scratch,
        compiler_params=params(mib),
        cost_estimate=pl.CostEstimate(flops=flops, bytes_accessed=moved, transcendentals=exps),
        name=name,
    )


def shape(dims, dtype=BF16):
    return jax.ShapeDtypeStruct(dims, dtype)


def local(
    queries,
    common_prefix_keys,
    common_prefix_values,
    branch_suffix_keys,
    branch_suffix_values,
    position_keys,
    position_values,
    lengths,
    out_weight,
):
    core = lax.rem(lax.axis_index("prefix"), 2).reshape(1)
    x = lax.rem(lax.axis_index("replica"), NX).reshape(1)
    z = (lax.axis_index("prefix") // 2 * 2 + lax.axis_index("replica") // NX).reshape(1)
    tensor = lax.axis_index("tensor").reshape(1)
    kv_rows = common_prefix_keys.shape[0]
    slots = branch_suffix_keys.shape[1]

    query_rows, query_flat = call(
        query_kernel, [shape((NZ, 64, HEAD)), shape((64, HEAD))], [VMEM], "query"
    )(queries.reshape(4, 2048))
    near_queries = lax.all_to_all(
        query_rows.reshape(2 * NZ, 32, HEAD),
        PLANE,
        0,
        0,
        tiled=True,
        axis_index_groups=ZC_GROUPS,
    ).reshape(NZ, 64, HEAD)

    send = pl.pallas_call(
        arrange_kernel,
        out_shape=shape((kv_rows, 2 * HEAD)),
        in_specs=[SMEM] + [pl.BlockSpec(memory_space=pltpu.HBM)] * 2,
        out_specs=pl.BlockSpec(memory_space=pltpu.HBM),
        scratch_shapes=[pltpu.SemaphoreType.DMA((2,))],
        compiler_params=params(),
        cost_estimate=pl.CostEstimate(
            flops=0, bytes_accessed=kv_rows * HEAD * 8, transcendentals=0
        ),
        name="arrange",
    )(core, common_prefix_keys, common_prefix_values)
    near_queries, send = lax.optimization_barrier((near_queries, send))
    other = call(
        fetch_kernel,
        shape((kv_rows, 2 * HEAD)),
        [pl.BlockSpec(memory_space=pl.ANY)],
        "fetch",
        moved=kv_rows * HEAD * 4,
        scratch=[pltpu.SemaphoreType.DMA],
    )(lax.ppermute(send, "prefix", CORE_SWAP))

    weight = out_weight.T
    width = weight.shape[1] // 2
    weight_send = lax.dynamic_slice_in_dim(weight, (1 - core[0]) * width, width, 1)
    weight_other = lax.ppermute(weight_send, "prefix", CORE_SWAP)

    own, own_send = call(
        suffix_kernel,
        [shape((64, HEAD), F32)] * 2,
        [SMEM] * 2 + [VMEM] * 5,
        "suffix",
        flops=2 * 32 * slots * HEAD * 4,
        moved=slots * HEAD * 8,
        exps=64 * slots,
    )(
        lengths,
        core,
        query_flat,
        branch_suffix_keys[0],
        branch_suffix_values[0],
        position_keys.reshape(4, 2 * HEAD),
        position_values.reshape(4, 2 * HEAD),
    )
    sibling = lax.ppermute(own_send, "prefix", CORE_SWAP)

    attend = call(
        functools.partial(attend_kernel, 512),
        shape(PACKED),
        [SMEM] + [VMEM] * 4,
        "attend",
        flops=4 * 512 * 2 * kv_rows * HEAD,
        moved=kv_rows * HEAD * 12,
        exps=512 * 2 * kv_rows,
        mib=16,
    )
    chunk_queries = [near_queries] + [
        lax.ppermute(near_queries, "replica", x_shift(-k)) for k in (1, 2, 3)
    ]
    partial = [
        attend(core, q, common_prefix_keys, common_prefix_values, other) for q in chunk_queries
    ]
    back = [lax.ppermute(partial[k], "replica", x_shift(k)) for k in (1, 2, 3)]
    merged = call(
        merge_kernel, shape(PACKED), [SMEM] * 2 + [VMEM] * 6, "merge", moved=6 * 135168
    )(z, core, partial[0], *back, own, sibling)
    for step in (0, 1):
        arrived = lax.ppermute(merged, PLANE, z_exchange(step))
        merged = call(pair_kernel, shape(PACKED), [VMEM] * 2, "pair")(merged, arrived)
    arrived = lax.ppermute(merged, PLANE, z_exchange(2))
    near_rows = call(finish_kernel, shape((64, 1024)), [VMEM] * 2, "finish")(merged, arrived)
    chunk_rows = [near_rows] + [
        lax.ppermute(near_rows, "replica", x_shift(-k)) for k in (1, 2, 3)
    ]
    columns = out_weight.shape[1]
    block = (NX, 16, columns)
    product, product_send = call(
        project_kernel,
        [shape((4,) + block)] * 2,
        [SMEM] * 2 + [VMEM] * 6,
        "project",
        flops=2 * 256 * 1024 * 160,
        moved=1 << 20,
    )(x, core, *chunk_rows, weight, weight_other)
    product_other = lax.ppermute(product_send, "prefix", CORE_SWAP)
    kept, sent = call(
        halve_kernel, [shape((2,) + block)] * 2, [SMEM] + [VMEM] * 2, "halve"
    )(tensor, product, product_other)
    arrived = lax.ppermute(sent, "tensor", [(t, t ^ 1) for t in range(4)])
    kept, sent = call(
        quarter_kernel, [shape(block, F32), shape(block)], [VMEM] * 2, "quarter"
    )(kept, arrived)
    arrived = lax.ppermute(sent, "tensor", [(t, 3 - t) for t in range(4)])
    return call(sum_kernel, shape((4, 16, columns)), [VMEM] * 2, "sum")(kept, arrived)


def solution(mesh):
    placed = (
        P(None, ("prefix", "replica"), "tensor"),
        P(("prefix", "replica"), "tensor"),
        P(("prefix", "replica"), "tensor"),
        P(("prefix", "replica"), None, "tensor"),
        P(("prefix", "replica"), None, "tensor"),
        P(None, ("prefix", "replica"), "tensor"),
        P(None, ("prefix", "replica"), "tensor"),
        P(("prefix", "replica")),
        P("tensor", ("prefix", "replica")),
    )
    return jax.shard_map(
        local,
        mesh=mesh,
        in_specs=placed,
        out_specs=P(None, "tensor", ("prefix", "replica")),
        check_vma=False,
    )
```

```python
import functools

import jax
import jax.numpy as jnp
from jax import lax
from jax.experimental import pallas as pl
from jax.experimental.pallas import tpu as pltpu
from jax.sharding import PartitionSpec as P

HEAD = 128
LOG2_SCALE = HEAD ** (-0.5) * 1.4426950408889634
NX, NZ = 4, 8
F32, BF16 = jnp.float32, jnp.bfloat16
PLANE = ("prefix", "replica")
VMEM = pl.BlockSpec(memory_space=pltpu.VMEM)
SMEM = pl.BlockSpec(memory_space=pltpu.SMEM)


def params(mib=8):
    return pltpu.CompilerParams(vmem_limit_bytes=mib << 20)


def plane_index(x, z, core):
    return ((z // 2) * 2 + core) * 8 + (z % 2) * 4 + x


ZC_GROUPS = [[plane_index(x, z, c) for z in range(NZ) for c in range(2)] for x in range(NX)]
CORE_SWAP = [(p, p ^ 1) for p in range(8)]


Z_PARTNERS = (
    [z ^ 1 for z in range(NZ)],
    [(z - 1) % NZ if z % 2 == 0 else (z + 1) % NZ for z in range(NZ)],
    [(z + 3) % NZ if z % 2 == 0 else (z - 3) % NZ for z in range(NZ)],
)


def z_exchange(step):
    return [
        (plane_index(x, z, c), plane_index(x, Z_PARTNERS[step][z], c))
        for x in range(NX)
        for z in range(NZ)
        for c in range(2)
    ]


def x_shift(k):
    return [(zl * 4 + x, zl * 4 + (x + k) % 4) for zl in range(2) for x in range(4)]


OUT_GROUPS = [
    [plane_index(x, z, c) * 4 + t for x in range(NX) for c in range(2) for t in range(4)]
    for z in range(NZ)
]


ROWS = NZ * 64
PACKED = (ROWS + 16, HEAD)


def eye():
    return lax.broadcasted_iota(jnp.int32, (HEAD, HEAD), 0) == lax.broadcasted_iota(
        jnp.int32, (HEAD, HEAD), 1
    )


def to_row(column):
    half = lax.broadcasted_iota(jnp.int32, (64, HEAD), 0)
    lane = lax.broadcasted_iota(jnp.int32, (64, HEAD), 1)
    low = jnp.where(half == lane, column[0:64], 0.0)
    high = jnp.where(half + 64 == lane, column[64:128], 0.0)
    return jnp.sum(low + high, axis=0, keepdims=True)


def pack(o_ref, parts):
    rows = []
    for i, (out, lse) in enumerate(parts):
        o_ref[i * HEAD : (i + 1) * HEAD, :] = out.astype(BF16)
        rows.append(to_row(lse))
    rows = jnp.concatenate(rows, axis=0)
    high = rows.astype(BF16).astype(F32)
    middle = (rows - high).astype(BF16).astype(F32)
    low = rows - high - middle
    stats = jnp.concatenate([high, middle, low, jnp.zeros_like(low)], axis=0)
    o_ref[ROWS:, :] = stats.astype(BF16)


def unpack(ref):
    stats = ref[ROWS:, :].astype(F32)
    rows = stats[0:4] + stats[4:8] + stats[8:12]
    parts = []
    for i in range(4):
        lse = jnp.sum(jnp.where(eye(), rows[i : i + 1], 0.0), axis=1, keepdims=True)
        parts.append((ref[i * HEAD : (i + 1) * HEAD, :].astype(F32), lse))
    return parts


def merge(parts):
    top = functools.reduce(jnp.maximum, [lse for _, lse in parts])
    factors = [jnp.exp2(lse - top) for _, lse in parts]
    total = functools.reduce(jnp.add, factors)
    summed = functools.reduce(jnp.add, [f * out for f, (out, _) in zip(factors, parts)])
    return summed / total, top + jnp.log2(total)


def query_kernel(q_ref, o_ref, flat_ref):
    q = q_ref[...].astype(F32)
    rows = jnp.concatenate([q[:, i * HEAD : (i + 1) * HEAD] for i in range(16)], axis=0)
    rows = rows.astype(BF16)
    flat_ref[...] = rows
    for z in range(NZ):
        o_ref[z] = rows


def arrange_kernel(core_ref, k_ref, v_ref, w_ref, send_ref, mine_ref, other_ref, sems):
    core = core_ref[0]
    width = mine_ref.shape[1]
    columns = pl.ds(pl.multiple_of((1 - core) * HEAD, HEAD), HEAD)
    pairs = [
        (k_ref.at[:, columns], send_ref.at[:, pl.ds(0, HEAD)]),
        (v_ref.at[:, columns], send_ref.at[:, pl.ds(HEAD, HEAD)]),
        (w_ref.at[:, pl.ds(pl.multiple_of(core * width, width), width)], mine_ref),
        (w_ref.at[:, pl.ds(pl.multiple_of((1 - core) * width, width), width)], other_ref),
    ]
    copies = [pltpu.make_async_copy(*pair, sems.at[i]) for i, pair in enumerate(pairs)]
    for copy in copies:
        copy.start()
    for copy in copies:
        copy.wait()


def stack_kernel(a_ref, b_ref, o_ref):
    rows = a_ref.shape[0]
    o_ref[:rows] = a_ref[...]
    o_ref[rows:] = b_ref[...]


def suffix_kernel(length_ref, core_ref, q_ref, k_ref, v_ref, nk_ref, nv_ref, own_ref, send_ref):
    length = length_ref[0]
    slots = k_ref.shape[0]
    visible = lax.broadcasted_iota(jnp.int32, (32, slots), 1) < length
    new_row = lax.broadcasted_iota(jnp.int32, (32, 16), 0) % 4
    new_col = lax.broadcasted_iota(jnp.int32, (32, 16), 1)
    causal = new_col <= new_row
    nt = (((1,), (1,)), ((), ()))
    empty = jnp.zeros((12, 2 * HEAD), F32)
    new_keys = jnp.concatenate([nk_ref[...].astype(F32), empty], axis=0).astype(BF16)
    new_values = jnp.concatenate([nv_ref[...].astype(F32), empty], axis=0).astype(BF16)
    results = []
    for g in range(2):
        columns = slice(g * HEAD, (g + 1) * HEAD)
        q = q_ref[g * 32 : (g + 1) * 32, :]
        s = lax.dot_general(q, k_ref[:, columns], nt, preferred_element_type=F32)
        t = lax.dot_general(q, new_keys[:, columns], nt, preferred_element_type=F32)
        s = jnp.where(visible, s * LOG2_SCALE, -jnp.inf)
        t = jnp.where(causal, t * LOG2_SCALE, -jnp.inf)
        top = jnp.maximum(
            jnp.max(s, axis=1, keepdims=True), jnp.max(t, axis=1, keepdims=True)
        )
        ws, wt = jnp.exp2(s - top), jnp.exp2(t - top)
        total = jnp.sum(ws, axis=1, keepdims=True) + jnp.sum(wt, axis=1, keepdims=True)
        summed = jnp.dot(ws.astype(BF16), v_ref[:, columns], preferred_element_type=F32)
        summed += jnp.dot(wt.astype(BF16), new_values[:, columns], preferred_element_type=F32)
        lse = jnp.broadcast_to(top + jnp.log2(total), (32, HEAD))
        results.append(jnp.concatenate([summed / total, lse], axis=0))
    first = core_ref[0] == 0
    own_ref[...] = jnp.where(first, results[0], results[1])
    send_ref[...] = jnp.where(first, results[1], results[0])


def fetch_kernel(away_ref, o_ref, sem):
    copy = pltpu.make_async_copy(away_ref, o_ref, sem)
    copy.start()
    copy.wait()


def attend_kernel(span, core_ref, q_ref, k_ref, v_ref, other_ref, o_ref):
    q = q_ref[...].reshape(NZ * 64, HEAD)
    top = summed = None
    mine = pl.ds(pl.multiple_of(core_ref[0] * HEAD, HEAD), HEAD)
    ones = jnp.ones((span, HEAD), BF16)
    sources = ((k_ref, mine, v_ref, mine), (other_ref, pl.ds(0, HEAD), other_ref, pl.ds(HEAD, HEAD)))
    for keys, key_columns, values, value_columns in sources:
        for start in range(0, keys.shape[0], span):
            rows = pl.ds(start, span)
            s = lax.dot_general(
                q,
                keys[rows, key_columns],
                (((1,), (1,)), ((), ())),
                preferred_element_type=F32,
            )
            here = jnp.max(s, axis=1, keepdims=True)
            new_top = here if top is None else jnp.maximum(top, here)
            w = jnp.exp2((s - new_top) * LOG2_SCALE).astype(BF16)
            widened = jnp.concatenate([values[rows, value_columns], ones], axis=1)
            part = jnp.dot(w, widened, preferred_element_type=F32)
            if top is None:
                summed = part
            else:
                summed = summed * jnp.exp2((top - new_top) * LOG2_SCALE) + part
            top = new_top
    total = summed[:, HEAD:]
    out = summed[:, :HEAD] / total
    lse = top * LOG2_SCALE + jnp.log2(total)
    blocks = [slice(i * HEAD, (i + 1) * HEAD) for i in range(4)]
    pack(o_ref, [(out[rows], lse[rows]) for rows in blocks])


def merge_kernel(z_ref, core_ref, a_ref, b_ref, c_ref, d_ref, own_ref, sibling_ref, o_ref):
    own, sibling = own_ref[...], sibling_ref[...]
    first = core_ref[0] == 0
    low, high = jnp.where(first, own, sibling), jnp.where(first, sibling, own)
    near_out = jnp.concatenate([low[0:32], high[0:32]] * 2, axis=0)
    near_lse = jnp.concatenate([low[32:], high[32:]] * 2, axis=0)
    half = lax.broadcasted_iota(jnp.int32, (HEAD, HEAD), 0) // 64
    far = [unpack(ref) for ref in (a_ref, b_ref, c_ref, d_ref)]
    merged = []
    for i in range(4):
        here = jnp.where(half + 2 * i == z_ref[0], near_lse, -jnp.inf)[:, 0:1]
        merged.append(merge([part[i] for part in far] + [(near_out, here)]))
    pack(o_ref, merged)


def pair_kernel(a_ref, b_ref, o_ref):
    pack(o_ref, [merge(list(parts)) for parts in zip(unpack(a_ref), unpack(b_ref))])


def finish(a_ref, b_ref):
    rows = []
    for parts in zip(unpack(a_ref), unpack(b_ref)):
        out, _ = merge(list(parts))
        for start in (0, 64):
            heads = [
                jnp.concatenate(
                    [
                        out[start + h * 4 : start + h * 4 + 4],
                        out[start + 32 + h * 4 : start + 36 + h * 4],
                    ],
                    axis=0,
                )
                for h in range(8)
            ]
            rows.append(jnp.concatenate(heads, axis=1))
    return jnp.concatenate(rows, axis=0).astype(BF16)


def project_kernel(x_ref, core_ref, a_ref, b_ref, *refs):
    *refs, o_ref = refs
    nt = (((1,), (1,)), ((), ()))
    rows = finish(a_ref, b_ref)
    width = refs[0].shape[0] // 2
    for k, ref in enumerate(refs):
        place = lax.rem(x_ref[0] + k, NX)
        for half, owner in enumerate((core_ref[0], 1 - core_ref[0])):
            weight = ref[half * width : (half + 1) * width, :]
            product = lax.dot_general(rows, weight, nt, preferred_element_type=F32)
            product = product.astype(BF16)
            for t in range(4):
                o_ref[place, owner, t] = product[t * 16 : (t + 1) * 16]


def sum_kernel(terms_ref, o_ref):
    total = []
    for x in range(NX):
        terms = [terms_ref[x * 8 + k].astype(F32) for k in range(8)]
        total.append(functools.reduce(jnp.add, terms))
    total = jnp.concatenate(total, axis=0)
    row = lax.broadcasted_iota(jnp.int32, (64, 64), 0)
    column = lax.broadcasted_iota(jnp.int32, (64, 64), 1)
    source = (row % 4) * 16 + ((row // 4) % 2) * 8 + ((row // 8) % 2) * 4 + row // 16
    moved = jnp.dot(
        (column == source).astype(BF16), total.astype(BF16), preferred_element_type=F32
    ).astype(BF16)
    for p in range(4):
        o_ref[p] = moved[p * 16 : (p + 1) * 16]


def call(kernel, shapes, specs, name, flops=0, moved=0, exps=0, mib=8, scratch=()):
    return pl.pallas_call(
        kernel,
        out_shape=shapes,
        in_specs=specs,
        out_specs=jax.tree.map(lambda _: VMEM, shapes),
        scratch_shapes=scratch,
        compiler_params=params(mib),
        cost_estimate=pl.CostEstimate(flops=flops, bytes_accessed=moved, transcendentals=exps),
        name=name,
    )


def shape(dims, dtype=BF16):
    return jax.ShapeDtypeStruct(dims, dtype)


def local(
    queries,
    common_prefix_keys,
    common_prefix_values,
    branch_suffix_keys,
    branch_suffix_values,
    position_keys,
    position_values,
    lengths,
    out_weight,
):
    core = lax.rem(lax.axis_index("prefix"), 2).reshape(1)
    x = lax.rem(lax.axis_index("replica"), NX).reshape(1)
    z = (lax.axis_index("prefix") // 2 * 2 + lax.axis_index("replica") // NX).reshape(1)
    kv_rows = common_prefix_keys.shape[0]
    slots = branch_suffix_keys.shape[1]

    query_rows, query_flat = call(
        query_kernel, [shape((NZ, 64, HEAD)), shape((64, HEAD))], [VMEM], "query"
    )(queries.reshape(4, 2048))
    near_queries = lax.all_to_all(
        query_rows.reshape(2 * NZ, 32, HEAD),
        PLANE,
        0,
        0,
        tiled=True,
        axis_index_groups=ZC_GROUPS,
    ).reshape(NZ, 64, HEAD)

    columns, width = out_weight.shape[1], out_weight.shape[0] // 2
    send, weight_mine, weight_send = pl.pallas_call(
        arrange_kernel,
        out_shape=[shape((kv_rows, 2 * HEAD))] + [shape((columns, width))] * 2,
        in_specs=[SMEM] + [pl.BlockSpec(memory_space=pltpu.HBM)] * 3,
        out_specs=[pl.BlockSpec(memory_space=pltpu.HBM)] + [VMEM] * 2,
        scratch_shapes=[pltpu.SemaphoreType.DMA((4,))],
        compiler_params=params(),
        cost_estimate=pl.CostEstimate(
            flops=0, bytes_accessed=kv_rows * HEAD * 8, transcendentals=0
        ),
        name="arrange",
    )(core, common_prefix_keys, common_prefix_values, out_weight.T)
    near_queries, send = lax.optimization_barrier((near_queries, send))
    other = call(
        fetch_kernel,
        shape((kv_rows, 2 * HEAD)),
        [pl.BlockSpec(memory_space=pl.ANY)],
        "fetch",
        moved=kv_rows * HEAD * 4,
        scratch=[pltpu.SemaphoreType.DMA],
    )(lax.ppermute(send, "prefix", CORE_SWAP))

    weight = call(stack_kernel, shape((2 * columns, width)), [VMEM] * 2, "stack")(
        weight_mine, lax.ppermute(weight_send, "prefix", CORE_SWAP)
    )
    weights = [weight] + [lax.ppermute(weight, "replica", x_shift(-k)) for k in (1, 2, 3)]

    own, own_send = call(
        suffix_kernel,
        [shape((64, HEAD), F32)] * 2,
        [SMEM] * 2 + [VMEM] * 5,
        "suffix",
        flops=2 * 32 * slots * HEAD * 4,
        moved=slots * HEAD * 8,
        exps=64 * slots,
    )(
        lengths,
        core,
        query_flat,
        branch_suffix_keys[0],
        branch_suffix_values[0],
        position_keys.reshape(4, 2 * HEAD),
        position_values.reshape(4, 2 * HEAD),
    )
    sibling = lax.ppermute(own_send, "prefix", CORE_SWAP)

    attend = call(
        functools.partial(attend_kernel, 256),
        shape(PACKED),
        [SMEM] + [VMEM] * 4,
        "attend",
        flops=4 * 512 * 2 * kv_rows * HEAD,
        moved=kv_rows * HEAD * 12,
        exps=512 * 2 * kv_rows,
        mib=16,
    )
    chunk_queries = [near_queries] + [
        lax.ppermute(near_queries, "replica", x_shift(-k)) for k in (1, 2, 3)
    ]
    partial = [
        attend(core, q, common_prefix_keys, common_prefix_values, other) for q in chunk_queries
    ]
    back = [lax.ppermute(partial[k], "replica", x_shift(k)) for k in (1, 2, 3)]
    merged = call(
        merge_kernel, shape(PACKED), [SMEM] * 2 + [VMEM] * 6, "merge", moved=6 * 135168
    )(z, core, partial[0], *back, own, sibling)
    for step in (0, 1):
        arrived = lax.ppermute(merged, PLANE, z_exchange(step))
        merged = call(pair_kernel, shape(PACKED), [VMEM] * 2, "pair")(merged, arrived)
    arrived = lax.ppermute(merged, PLANE, z_exchange(2))
    product = call(
        project_kernel,
        shape((NX, 2, 4, 16, columns)),
        [SMEM] * 2 + [VMEM] * 6,
        "project",
        flops=2 * 64 * 1024 * 640,
        moved=2 << 20,
    )(x, core, merged, arrived, *weights)
    terms = lax.all_to_all(
        product.reshape(NX * 8, 16, columns),
        PLANE + ("tensor",),
        0,
        0,
        tiled=True,
        axis_index_groups=OUT_GROUPS,
    )
    return call(sum_kernel, shape((4, 16, columns)), [VMEM], "sum")(terms)


def solution(mesh):
    placed = (
        P(None, ("prefix", "replica"), "tensor"),
        P(("prefix", "replica"), "tensor"),
        P(("prefix", "replica"), "tensor"),
        P(("prefix", "replica"), None, "tensor"),
        P(("prefix", "replica"), None, "tensor"),
        P(None, ("prefix", "replica"), "tensor"),
        P(None, ("prefix", "replica"), "tensor"),
        P(("prefix", "replica")),
        P("tensor", ("prefix", "replica")),
    )
    return jax.shard_map(
        local,
        mesh=mesh,
        in_specs=placed,
        out_specs=P(None, "tensor", ("prefix", "replica")),
        check_vma=False,
    )
```

```python
import functools

import jax
import jax.numpy as jnp
from jax import lax
from jax.experimental import pallas as pl
from jax.experimental.pallas import tpu as pltpu
from jax.sharding import PartitionSpec as P

HEAD = 128
LOG2_SCALE = HEAD ** (-0.5) * 1.4426950408889634
NX, NZ = 4, 8
F32, BF16 = jnp.float32, jnp.bfloat16
PLANE = ("prefix", "replica")
VMEM = pl.BlockSpec(memory_space=pltpu.VMEM)
SMEM = pl.BlockSpec(memory_space=pltpu.SMEM)


def params(mib=8):
    return pltpu.CompilerParams(vmem_limit_bytes=mib << 20)


def plane_index(x, z, core):
    return ((z // 2) * 2 + core) * 8 + (z % 2) * 4 + x


ZC_GROUPS = [[plane_index(x, z, c) for z in range(NZ) for c in range(2)] for x in range(NX)]
CORE_SWAP = [(p, p ^ 1) for p in range(8)]


Z_PARTNERS = (
    [z ^ 1 for z in range(NZ)],
    [(z - 1) % NZ if z % 2 == 0 else (z + 1) % NZ for z in range(NZ)],
    [(z + 3) % NZ if z % 2 == 0 else (z - 3) % NZ for z in range(NZ)],
)


def z_exchange(step):
    return [
        (plane_index(x, z, c), plane_index(x, Z_PARTNERS[step][z], c))
        for x in range(NX)
        for z in range(NZ)
        for c in range(2)
    ]


def x_shift(k):
    return [(zl * 4 + x, zl * 4 + (x + k) % 4) for zl in range(2) for x in range(4)]


OUT_GROUPS = [
    [plane_index(x, z, c) * 4 + t for x in range(NX) for t in range(4)]
    for z in range(NZ)
    for c in range(2)
]


ROWS = NZ * 64
PACKED = (ROWS + 16, HEAD)


def eye():
    return lax.broadcasted_iota(jnp.int32, (HEAD, HEAD), 0) == lax.broadcasted_iota(
        jnp.int32, (HEAD, HEAD), 1
    )


def to_row(column):
    half = lax.broadcasted_iota(jnp.int32, (64, HEAD), 0)
    lane = lax.broadcasted_iota(jnp.int32, (64, HEAD), 1)
    low = jnp.where(half == lane, column[0:64], 0.0)
    high = jnp.where(half + 64 == lane, column[64:128], 0.0)
    return jnp.sum(low + high, axis=0, keepdims=True)


def pack(o_ref, parts):
    rows = []
    for i, (out, lse) in enumerate(parts):
        o_ref[i * HEAD : (i + 1) * HEAD, :] = out.astype(BF16)
        rows.append(to_row(lse))
    rows = jnp.concatenate(rows, axis=0)
    high = rows.astype(BF16).astype(F32)
    middle = (rows - high).astype(BF16).astype(F32)
    low = rows - high - middle
    stats = jnp.concatenate([high, middle, low, jnp.zeros_like(low)], axis=0)
    o_ref[ROWS:, :] = stats.astype(BF16)


def unpack(ref):
    stats = ref[ROWS:, :].astype(F32)
    rows = stats[0:4] + stats[4:8] + stats[8:12]
    parts = []
    for i in range(4):
        lse = jnp.sum(jnp.where(eye(), rows[i : i + 1], 0.0), axis=1, keepdims=True)
        parts.append((ref[i * HEAD : (i + 1) * HEAD, :].astype(F32), lse))
    return parts


def merge(parts):
    top = functools.reduce(jnp.maximum, [lse for _, lse in parts])
    factors = [jnp.exp2(lse - top) for _, lse in parts]
    total = functools.reduce(jnp.add, factors)
    summed = functools.reduce(jnp.add, [f * out for f, (out, _) in zip(factors, parts)])
    return summed / total, top + jnp.log2(total)


def query_kernel(q_ref, o_ref, flat_ref, held_ref, sem):
    copy = pltpu.make_async_copy(q_ref, held_ref, sem)
    copy.start()
    copy.wait()
    q = held_ref[...].reshape(4, 16 * HEAD).astype(F32)
    rows = jnp.concatenate([q[:, i * HEAD : (i + 1) * HEAD] for i in range(16)], axis=0)
    rows = rows.astype(BF16)
    flat_ref[...] = rows
    for z in range(NZ):
        o_ref[z] = rows


def arrange_kernel(core_ref, k_ref, v_ref, w_ref, send_ref, mine_ref, other_ref, sems):
    core = core_ref[0]
    width = mine_ref.shape[1]
    columns = pl.ds(pl.multiple_of((1 - core) * HEAD, HEAD), HEAD)
    pairs = [
        (k_ref.at[:, columns], send_ref.at[:, pl.ds(0, HEAD)]),
        (v_ref.at[:, columns], send_ref.at[:, pl.ds(HEAD, HEAD)]),
        (w_ref.at[:, pl.ds(pl.multiple_of(core * width, width), width)], mine_ref),
        (w_ref.at[:, pl.ds(pl.multiple_of((1 - core) * width, width), width)], other_ref),
    ]
    copies = [pltpu.make_async_copy(*pair, sems.at[i]) for i, pair in enumerate(pairs)]
    for copy in copies:
        copy.start()
    for copy in copies:
        copy.wait()


def stack_kernel(a_ref, b_ref, o_ref):
    rows = a_ref.shape[0]
    o_ref[:rows] = a_ref[...]
    o_ref[rows:] = b_ref[...]


def suffix_kernel(length_ref, core_ref, q_ref, k_ref, v_ref, nk_ref, nv_ref, own_ref, send_ref):
    length = length_ref[0]
    slots = k_ref.shape[0]
    visible = lax.broadcasted_iota(jnp.int32, (32, slots), 1) < length
    new_row = lax.broadcasted_iota(jnp.int32, (32, 16), 0) % 4
    new_col = lax.broadcasted_iota(jnp.int32, (32, 16), 1)
    causal = new_col <= new_row
    nt = (((1,), (1,)), ((), ()))
    empty = jnp.zeros((12, 2 * HEAD), F32)
    new_keys = jnp.concatenate([nk_ref[...].astype(F32), empty], axis=0).astype(BF16)
    new_values = jnp.concatenate([nv_ref[...].astype(F32), empty], axis=0).astype(BF16)
    results = []
    for g in range(2):
        columns = slice(g * HEAD, (g + 1) * HEAD)
        q = q_ref[g * 32 : (g + 1) * 32, :]
        s = lax.dot_general(q, k_ref[:, columns], nt, preferred_element_type=F32)
        t = lax.dot_general(q, new_keys[:, columns], nt, preferred_element_type=F32)
        s = jnp.where(visible, s * LOG2_SCALE, -jnp.inf)
        t = jnp.where(causal, t * LOG2_SCALE, -jnp.inf)
        top = jnp.maximum(
            jnp.max(s, axis=1, keepdims=True), jnp.max(t, axis=1, keepdims=True)
        )
        ws, wt = jnp.exp2(s - top), jnp.exp2(t - top)
        total = jnp.sum(ws, axis=1, keepdims=True) + jnp.sum(wt, axis=1, keepdims=True)
        summed = jnp.dot(ws.astype(BF16), v_ref[:, columns], preferred_element_type=F32)
        summed += jnp.dot(wt.astype(BF16), new_values[:, columns], preferred_element_type=F32)
        lse = jnp.broadcast_to(top + jnp.log2(total), (32, HEAD))
        results.append(jnp.concatenate([summed / total, lse], axis=0))
    first = core_ref[0] == 0
    own_ref[...] = jnp.where(first, results[0], results[1])
    send_ref[...] = jnp.where(first, results[1], results[0])


def fetch_kernel(away_ref, o_ref, sem):
    copy = pltpu.make_async_copy(away_ref, o_ref, sem)
    copy.start()
    copy.wait()


def attend_kernel(span, core_ref, q_ref, k_ref, v_ref, other_ref, o_ref):
    q = q_ref[...].reshape(NZ * 64, HEAD)
    top = summed = None
    mine = pl.ds(pl.multiple_of(core_ref[0] * HEAD, HEAD), HEAD)
    ones = jnp.ones((span, HEAD), BF16)
    sources = ((k_ref, mine, v_ref, mine), (other_ref, pl.ds(0, HEAD), other_ref, pl.ds(HEAD, HEAD)))
    for keys, key_columns, values, value_columns in sources:
        for start in range(0, keys.shape[0], span):
            rows = pl.ds(start, span)
            s = lax.dot_general(
                q,
                keys[rows, key_columns],
                (((1,), (1,)), ((), ())),
                preferred_element_type=F32,
            )
            here = jnp.max(s, axis=1, keepdims=True)
            new_top = here if top is None else jnp.maximum(top, here)
            w = jnp.exp2((s - new_top) * LOG2_SCALE).astype(BF16)
            widened = jnp.concatenate([values[rows, value_columns], ones], axis=1)
            part = jnp.dot(w, widened, preferred_element_type=F32)
            if top is None:
                summed = part
            else:
                summed = summed * jnp.exp2((top - new_top) * LOG2_SCALE) + part
            top = new_top
    total = summed[:, HEAD:]
    out = summed[:, :HEAD] / total
    lse = top * LOG2_SCALE + jnp.log2(total)
    blocks = [slice(i * HEAD, (i + 1) * HEAD) for i in range(4)]
    pack(o_ref, [(out[rows], lse[rows]) for rows in blocks])


def merge_kernel(z_ref, core_ref, a_ref, b_ref, c_ref, d_ref, own_ref, sibling_ref, o_ref):
    own, sibling = own_ref[...], sibling_ref[...]
    first = core_ref[0] == 0
    low, high = jnp.where(first, own, sibling), jnp.where(first, sibling, own)
    near_out = jnp.concatenate([low[0:32], high[0:32]] * 2, axis=0)
    near_lse = jnp.concatenate([low[32:], high[32:]] * 2, axis=0)
    half = lax.broadcasted_iota(jnp.int32, (HEAD, HEAD), 0) // 64
    far = [unpack(ref) for ref in (a_ref, b_ref, c_ref, d_ref)]
    merged = []
    for i in range(4):
        here = jnp.where(half + 2 * i == z_ref[0], near_lse, -jnp.inf)[:, 0:1]
        merged.append(merge([part[i] for part in far] + [(near_out, here)]))
    pack(o_ref, merged)


def pair_kernel(a_ref, b_ref, o_ref):
    pack(o_ref, [merge(list(parts)) for parts in zip(unpack(a_ref), unpack(b_ref))])


def finish(a_ref, b_ref):
    rows = []
    for parts in zip(unpack(a_ref), unpack(b_ref)):
        out, _ = merge(list(parts))
        for start in (0, 64):
            heads = [
                jnp.concatenate(
                    [
                        out[start + h * 4 : start + h * 4 + 4],
                        out[start + 32 + h * 4 : start + 36 + h * 4],
                    ],
                    axis=0,
                )
                for h in range(8)
            ]
            rows.append(jnp.concatenate(heads, axis=1))
    return jnp.concatenate(rows, axis=0).astype(BF16)


def project_kernel(x_ref, a_ref, b_ref, *refs):
    *refs, own_ref, send_ref = refs
    nt = (((1,), (1,)), ((), ()))
    rows = finish(a_ref, b_ref)
    width = refs[0].shape[0] // 2
    for k, ref in enumerate(refs):
        place = lax.rem(x_ref[0] + k, NX)
        for half, o_ref in enumerate((own_ref, send_ref)):
            weight = ref[half * width : (half + 1) * width, :]
            product = lax.dot_general(rows, weight, nt, preferred_element_type=F32)
            product = product.astype(BF16)
            for t in range(4):
                o_ref[place, t] = product[t * 16 : (t + 1) * 16]


def add_kernel(a_ref, b_ref, o_ref):
    o_ref[...] = (a_ref[...].astype(F32) + b_ref[...].astype(F32)).astype(BF16)


def sum_kernel(terms_ref, o_ref):
    total = []
    for x in range(NX):
        terms = [terms_ref[x * 4 + k].astype(F32) for k in range(4)]
        total.append(functools.reduce(jnp.add, terms))
    total = jnp.concatenate(total, axis=0)
    row = lax.broadcasted_iota(jnp.int32, (64, 64), 0)
    column = lax.broadcasted_iota(jnp.int32, (64, 64), 1)
    source = (row % 4) * 16 + ((row // 4) % 2) * 8 + ((row // 8) % 2) * 4 + row // 16
    moved = jnp.dot(
        (column == source).astype(BF16), total.astype(BF16), preferred_element_type=F32
    ).astype(BF16)
    for p in range(4):
        o_ref[p] = moved[p * 16 : (p + 1) * 16]


def call(kernel, shapes, specs, name, flops=0, moved=0, exps=0, mib=8, scratch=()):
    return pl.pallas_call(
        kernel,
        out_shape=shapes,
        in_specs=specs,
        out_specs=jax.tree.map(lambda _: VMEM, shapes),
        scratch_shapes=scratch,
        compiler_params=params(mib),
        cost_estimate=pl.CostEstimate(flops=flops, bytes_accessed=moved, transcendentals=exps),
        name=name,
    )


def shape(dims, dtype=BF16):
    return jax.ShapeDtypeStruct(dims, dtype)


def local(
    queries,
    common_prefix_keys,
    common_prefix_values,
    branch_suffix_keys,
    branch_suffix_values,
    position_keys,
    position_values,
    lengths,
    out_weight,
):
    core = lax.rem(lax.axis_index("prefix"), 2).reshape(1)
    x = lax.rem(lax.axis_index("replica"), NX).reshape(1)
    z = (lax.axis_index("prefix") // 2 * 2 + lax.axis_index("replica") // NX).reshape(1)
    kv_rows = common_prefix_keys.shape[0]
    slots = branch_suffix_keys.shape[1]

    query_rows, query_flat = call(
        query_kernel,
        [shape((NZ, 64, HEAD)), shape((64, HEAD))],
        [pl.BlockSpec(memory_space=pl.ANY)],
        "query",
        scratch=[pltpu.VMEM((4, 1, 2048), BF16), pltpu.SemaphoreType.DMA],
    )(queries)
    near_queries = lax.all_to_all(
        query_rows.reshape(2 * NZ, 32, HEAD),
        PLANE,
        0,
        0,
        tiled=True,
        axis_index_groups=ZC_GROUPS,
    ).reshape(NZ, 64, HEAD)

    columns, width = out_weight.shape[1], out_weight.shape[0] // 2
    send, weight_mine, weight_send = pl.pallas_call(
        arrange_kernel,
        out_shape=[shape((kv_rows, 2 * HEAD))] + [shape((columns, width))] * 2,
        in_specs=[SMEM] + [pl.BlockSpec(memory_space=pltpu.HBM)] * 3,
        out_specs=[pl.BlockSpec(memory_space=pltpu.HBM)] + [VMEM] * 2,
        scratch_shapes=[pltpu.SemaphoreType.DMA((4,))],
        compiler_params=params(),
        cost_estimate=pl.CostEstimate(
            flops=0, bytes_accessed=kv_rows * HEAD * 8, transcendentals=0
        ),
        name="arrange",
    )(core, common_prefix_keys, common_prefix_values, out_weight.T)
    near_queries, send = lax.optimization_barrier((near_queries, send))
    other = call(
        fetch_kernel,
        shape((kv_rows, 2 * HEAD)),
        [pl.BlockSpec(memory_space=pl.ANY)],
        "fetch",
        moved=kv_rows * HEAD * 4,
        scratch=[pltpu.SemaphoreType.DMA],
    )(lax.ppermute(send, "prefix", CORE_SWAP))

    weight = call(stack_kernel, shape((2 * columns, width)), [VMEM] * 2, "stack")(
        weight_mine, lax.ppermute(weight_send, "prefix", CORE_SWAP)
    )
    weights = [weight] + [lax.ppermute(weight, "replica", x_shift(-k)) for k in (1, 2, 3)]

    own, own_send = call(
        suffix_kernel,
        [shape((64, HEAD), F32)] * 2,
        [SMEM] * 2 + [VMEM] * 5,
        "suffix",
        flops=2 * 32 * slots * HEAD * 4,
        moved=slots * HEAD * 8,
        exps=64 * slots,
    )(
        lengths,
        core,
        query_flat,
        branch_suffix_keys[0],
        branch_suffix_values[0],
        position_keys.reshape(4, 2 * HEAD),
        position_values.reshape(4, 2 * HEAD),
    )
    sibling = lax.ppermute(own_send, "prefix", CORE_SWAP)

    attend = call(
        functools.partial(attend_kernel, 256),
        shape(PACKED),
        [SMEM] + [VMEM] * 4,
        "attend",
        flops=4 * 512 * 2 * kv_rows * HEAD,
        moved=kv_rows * HEAD * 12,
        exps=512 * 2 * kv_rows,
        mib=16,
    )
    chunk_queries = [near_queries] + [
        lax.ppermute(near_queries, "replica", x_shift(-k)) for k in (1, 2, 3)
    ]
    partial = [
        attend(core, q, common_prefix_keys, common_prefix_values, other) for q in chunk_queries
    ]
    back = [lax.ppermute(partial[k], "replica", x_shift(k)) for k in (1, 2, 3)]
    merged = call(
        merge_kernel, shape(PACKED), [SMEM] * 2 + [VMEM] * 6, "merge", moved=6 * 135168
    )(z, core, partial[0], *back, own, sibling)
    for step in (0, 1):
        arrived = lax.ppermute(merged, PLANE, z_exchange(step))
        merged = call(pair_kernel, shape(PACKED), [VMEM] * 2, "pair")(merged, arrived)
    arrived = lax.ppermute(merged, PLANE, z_exchange(2))
    block = (NX, 4, 16, columns)
    product, product_send = call(
        project_kernel,
        [shape(block)] * 2,
        [SMEM] + [VMEM] * 6,
        "project",
        flops=2 * 64 * 1024 * 640,
        moved=2 << 20,
    )(x, merged, arrived, *weights)
    product = call(add_kernel, shape(block), [VMEM] * 2, "add")(
        product, lax.ppermute(product_send, "prefix", CORE_SWAP)
    )
    terms = lax.all_to_all(
        product.reshape(NX * 4, 16, columns),
        PLANE + ("tensor",),
        0,
        0,
        tiled=True,
        axis_index_groups=OUT_GROUPS,
    )
    return call(sum_kernel, shape((4, 16, columns)), [VMEM], "sum")(terms)


def solution(mesh):
    placed = (
        P(None, ("prefix", "replica"), "tensor"),
        P(("prefix", "replica"), "tensor"),
        P(("prefix", "replica"), "tensor"),
        P(("prefix", "replica"), None, "tensor"),
        P(("prefix", "replica"), None, "tensor"),
        P(None, ("prefix", "replica"), "tensor"),
        P(None, ("prefix", "replica"), "tensor"),
        P(("prefix", "replica")),
        P("tensor", ("prefix", "replica")),
    )
    return jax.shard_map(
        local,
        mesh=mesh,
        in_specs=placed,
        out_specs=P(None, "tensor", ("prefix", "replica")),
        check_vma=False,
    )
```
